32 devices in a mesh: layer: 8 (over z, y), feat: 4 (over x, core).
Axes of the slice: x: 2, y: 2, z: 4, core: 2. Of those that a mesh axis runs over, the one named last changes fastest.
Arguments:
- sources: bfloat16 [32, 8192], P(('layer', 'feat')), may hold values from -6 to 6
- targets: bfloat16 [32, 16384], P(('layer', 'feat')), may hold values from -16 to 16
- enc_weight: bfloat16 [8192, 32768], P(None, ('feat', 'layer')), may hold values from -0.0625 to 0.0625
- enc_bias: float32 [32768], P(('feat', 'layer')), may hold values from -3 to 3
- dec_weight: bfloat16 [32768, 16384], P('feat', 'layer'), may hold values from -0.03125 to 0.03125
- dec_bias: float32 [16384], P('layer'), may hold values from -3 to 3
Outputs:
- enc_grad: bfloat16 [8192, 32768], P(None, ('feat', 'layer'))
- dec_grad: bfloat16 [32768, 16384], P('feat', 'layer')
- mse: float32 [], replicated
The draws below stay inside these ranges and needn't reach their ends.
All inputs are finite; a program needn't handle non-finite values.
Results may differ from the reference program's by a relative error of at most 0.011.
Values may be sent and summed in bfloat16 or wider, within the bound.
A program may use at most 192 MiB of HBM per device.

```python
import math
import jax
import jax.numpy as jnp
from jax import lax

D = 8192
F = 32768
TL = 2
TOKENS = 32


def draw_targets(key, part):
    columns = TL * D
    place = jnp.arange(columns, dtype=jnp.float32) / float(columns - 1)
    scale = jnp.exp(place * jnp.log(3.5))
    base = jnp.clip(jax.random.normal(key, (TOKENS, columns), jnp.float32), -4.0, 4.0)
    return (base * scale[None, :]).astype(jnp.bfloat16)


def level_of(rng, dims, shards, low, top_value):
    loudness, own = 1.0, jax.random.fold_in(rng, 6)
    for axis_at, shards_of in shards:
        heights = jnp.exp(jax.random.uniform(jax.random.fold_in(own, axis_at), (shards_of,), jnp.float32, low / len(shards), top_value / len(shards)))
        loudness = loudness * jnp.repeat(heights, dims[axis_at] // shards_of).reshape([-1 if axis == axis_at else 1 for axis in range(len(dims))])
    return loudness


def gaussian(key, dims, scale, limit, cuts=(), held_as=jnp.bfloat16):
    loudness = level_of(key, dims, cuts, -0.22, 0.18) if cuts else 1.0
    array = jax.random.normal(key, dims, jnp.float32) * scale * loudness
    return jnp.minimum(jnp.maximum(array, -limit), limit).astype(held_as)


def setup_inputs(seed: int = 0) -> dict:
    key_list = jax.random.split(jax.random.key(seed), 7)
    return {
        "sources": gaussian(key_list[0], (TOKENS, D), 1.0, 6.0, ((0, 32),)),
        "targets": draw_targets(jax.random.fold_in(key_list[6], 71), 0),
        "enc_weight": gaussian(key_list[2], (D, F), D ** -0.5, 0.0625, ((1, 32),)),
        "enc_bias": gaussian(key_list[3], (F,), 0.5, 3.0, ((0, 32),), jnp.float32),
        "dec_weight": gaussian(key_list[4], (F, TL * D), F ** -0.5, 0.03125, ((0, 4), (1, 8))),
        "dec_bias": gaussian(key_list[5], (TL * D,), 0.5, 3.0, ((0, 8),), jnp.float32),
    }


def column_blocks(left, right):
    width = right.shape[1]
    size = 1024 if width % 1024 == 0 else width
    count = width // size
    parts = right.reshape(right.shape[0], count, size).transpose(1, 0, 2)

    def one_block(part):
        return lax.dot_general(left, part, (((0,), (0,)), ((), ())), preferred_element_type=jnp.float32).astype(jnp.bfloat16)
    stacked = lax.map(one_block, parts)
    return stacked.transpose(1, 0, 2).reshape(left.shape[1], width)

def reference(sources, targets, enc_weight, enc_bias, dec_weight, dec_bias):
    preact = jnp.dot(sources, enc_weight, preferred_element_type=jnp.float32) + enc_bias
    feats = jax.nn.gelu(preact).astype(jnp.bfloat16)
    outputs = jnp.dot(feats, dec_weight, preferred_element_type=jnp.float32) + dec_bias
    misfit = outputs - targets.astype(jnp.float32)
    errors = (misfit * (1.0 / math.sqrt(TOKENS))).astype(jnp.bfloat16)
    mse = jnp.sum(misfit * misfit) / (TOKENS * TL * D)
    dec_grad = column_blocks(feats, errors)
    feat_grad = lax.dot_general(errors, dec_weight, (((1,), (1,)), ((), ())), preferred_element_type=jnp.float32)
    _, pullback = jax.vjp(jax.nn.gelu, preact)
    pre_grad = pullback(feat_grad)[0].astype(jnp.bfloat16)
    enc_grad = column_blocks(sources, pre_grad)
    return (enc_grad, dec_grad, mse)
```

```python
import functools
import math

import jax
import jax.numpy as jnp
from jax import lax
from jax.experimental import pallas as pl
from jax.experimental.pallas import tpu as pltpu
from jax.sharding import PartitionSpec as P

MESH = pl.DeviceIdType.MESH
BF16 = jnp.bfloat16
F32 = jnp.float32
LANES = 128


def split2(n):
    return (n // 2, 2) if n % 2 == 0 else (n, 1)


def gather_kernel(
    nl, nf, scale, mse_scale,
    src_ref, tgt_ref, ebias_ref, dbias_ref, ew_hbm, dw_hbm,
    x_out, feats_out, err_out, pre_out, mse_out,
    ew, dw, rows, rows32, tgts, tgt32, preact, part, rs_send, rs_recv, err,
    g_send1, g_recv1, g_send2, g_recv2, sq_send, sq_recv, tot_send, tot_recv,
    ew_sem, dw_sem,
    s1_send, s1_recv, s2_send, s2_recv, s3_send, s3_recv, t_send, t_recv,
    fa_send, fa_recv, fb_send, fb_recv, rs_ssem, rs_rsem, er_send, er_recv,
    q1_send, q1_recv, q2_send, q2_recv, sq_ssem, sq_rsem, tt_ssem, tt_rsem,
):
    lo_n, li_n = split2(nl)
    fo_n, fi_n = split2(nf)
    l = lax.axis_index("layer")
    f = lax.axis_index("feat")
    lo, li = l // li_n, l % li_n
    fo, fi = f // fi_n, f % fi_n
    nk, tokens, kw = x_out.shape
    fl = feats_out.shape[2]
    tf = tokens // nf
    width = dw.shape[1]

    for k in range(nk):
        pltpu.make_async_copy(ew_hbm.at[pl.ds(k * kw, kw)], ew.at[pl.ds(k * kw, kw)], ew_sem.at[k]).start()

    def dw_copy(c):
        sl = pl.ds(pl.multiple_of(c * fl, fl), fl)
        return pltpu.make_async_copy(dw_hbm.at[sl], dw.at[sl], dw_sem.at[c])

    barrier = pltpu.get_barrier_semaphore()
    for d in range(1, nl):
        pl.semaphore_signal(barrier, inc=1, device_id=((l + d) % nl, f), device_id_type=MESH)
    for d in range(1, nf):
        pl.semaphore_signal(barrier, inc=1, device_id=(l, (f + d) % nf), device_id_type=MESH)
    pl.semaphore_wait(barrier, nl - 1 + nf - 1)

    def remote(src, dst, ssem, rsem, dev):
        return pltpu.make_async_remote_copy(
            src_ref=src, dst_ref=dst, send_sem=ssem, recv_sem=rsem, device_id=dev, device_id_type=MESH
        )

    sends = []

    def send(src, dst, ssem, rsem, dev):
        c = remote(src, dst, ssem, rsem, dev)
        c.start()
        sends.append(c)

    rows[f, l] = src_ref[...]
    for d in range(1, nl):
        to = (l + d) % nl
        send(rows.at[f, l], rows.at[f, l], s1_send.at[d], s1_recv.at[d], (to, f))
    for d in range(1, nl):
        to = (l + d) % nl
        send(tgt_ref.at[to], tgts.at[l], t_send.at[d], t_recv.at[d], (to, f))
    for c in range(nl):
        dw_copy(c).start()
    for d in range(1, nl):
        frm = (l - d + nl) % nl
        remote(rows.at[f, frm], rows.at[f, frm], s1_send.at[d], s1_recv.at[d], (frm, f)).wait_recv()
    for d in range(1, fo_n):
        to = ((fo + d) % fo_n) * fi_n + fi
        send(rows.at[f], rows.at[f], s2_send.at[d], s2_recv.at[d], (l, to))
    if fi_n == 2:
        peer = fo * fi_n + 1 - fi
        send(rows.at[f], rows.at[f], s3_send.at[0], s3_recv.at[0], (l, peer))
    for d in range(1, fo_n):
        b = ((fo - d + fo_n) % fo_n) * fi_n + fi
        remote(rows.at[b], rows.at[b], s2_send.at[d], s2_recv.at[d], (l, b)).wait_recv()
        if fi_n == 2:
            send(rows.at[b], rows.at[b], s3_send.at[d], s3_recv.at[d], (l, peer))
    if fi_n == 2:
        for d in range(fo_n):
            b = ((fo - d + fo_n) % fo_n) * fi_n + 1 - fi
            remote(rows.at[b], rows.at[b], s3_send.at[d], s3_recv.at[d], (l, peer)).wait_recv()
    per = nk * kw // LANES
    rows32[...] = rows[...].astype(F32).reshape(tokens * per, LANES)
    for s in range(per):
        at = s * LANES
        x_out[at // kw, :, at % kw : at % kw + LANES] = rows32[pl.ds(s, tokens, stride=per), :].astype(BF16)

    preact[...] = jnp.broadcast_to(ebias_ref[...], preact.shape)

    def enc_step(k, _):
        sl = pl.ds(pl.multiple_of(k * kw, kw), kw)
        pltpu.make_async_copy(ew_hbm.at[sl], ew.at[sl], ew_sem.at[k]).wait()
        preact[...] += jnp.dot(x_out[k], ew[sl, :], preferred_element_type=F32)
        return 0

    lax.fori_loop(0, nk, enc_step, 0)
    feats_out[l] = jax.nn.gelu(preact[...]).astype(BF16)

    for d in range(1, lo_n):
        to = ((lo + d) % lo_n) * li_n + li
        send(feats_out.at[l], feats_out.at[l], fa_send.at[d], fa_recv.at[d], (to, f))
    lpeer = lo * li_n + 1 - li
    if li_n == 2:
        send(feats_out.at[l], feats_out.at[l], fb_send.at[0], fb_recv.at[0], (lpeer, f))
    part[...] = jnp.zeros_like(part)

    def decode(c):
        dw_copy(c).wait()
        sl = pl.ds(pl.multiple_of(c * fl, fl), fl)
        part[...] += jnp.dot(feats_out[c], dw[sl, :], preferred_element_type=F32)

    def dec_step(d, _):
        b = ((lo - d + lo_n) % lo_n) * li_n + li

        @pl.when(d > 0)
        def _():
            remote(feats_out.at[b], feats_out.at[b], fa_send.at[d], fa_recv.at[d], (b, f)).wait_recv()
            if li_n == 2:
                remote(feats_out.at[b], feats_out.at[b], fb_send.at[d], fb_recv.at[d], (lpeer, f)).start()

        decode(b)
        return 0

    lax.fori_loop(0, lo_n, dec_step, 0)
    if li_n == 2:

        def dec_step2(d, _):
            b = ((lo - d + lo_n) % lo_n) * li_n + 1 - li
            remote(feats_out.at[b], feats_out.at[b], fb_send.at[d], fb_recv.at[d], (lpeer, f)).wait_recv()
            decode(b)
            return 0

        lax.fori_loop(0, lo_n, dec_step2, 0)

    tgts[l] = tgt_ref[l]
    for d in range(1, nl):
        frm = (l - d + nl) % nl
        remote(tgts.at[frm], tgts.at[frm], t_send.at[d], t_recv.at[d], (frm, f)).wait_recv()
    cper = width // LANES
    tgt32[...] = tgts[...].astype(F32).reshape(tf * cper, LANES)

    rs_send[...] = part[...].reshape(nf, tf, width).astype(BF16)
    for d in range(1, nf):
        to = (f + d) % nf
        send(rs_send.at[to], rs_recv.at[d], rs_ssem.at[d], rs_rsem.at[d], (l, to))
    own = part[pl.ds(pl.multiple_of(f * tf, tf), tf), :]
    own = own + dbias_ref[...]
    want = jnp.concatenate([tgt32[pl.ds(s, tf, stride=cper), :] for s in range(cper)], axis=1)
    for d in range(1, nf):
        remote(rs_recv.at[d], rs_recv.at[d], rs_ssem.at[d], rs_rsem.at[d], (l, f)).wait_recv()
        own = own + rs_recv[d].astype(F32)
    misfit = own - want
    err[f] = (misfit * scale).astype(BF16)
    for d in range(1, nf):
        to = (f + d) % nf
        send(err.at[f], err.at[f], er_send.at[d], er_recv.at[d], (l, to))
    sq = jnp.sum(misfit * misfit)
    sq_send[...] = jnp.full(sq_send.shape, sq, F32)
    for d in range(1, nf):
        to = (f + d) % nf
        send(sq_send, sq_recv.at[d], sq_ssem.at[d], sq_rsem.at[d], (l, to))
    for d in range(1, nf):
        frm = (f - d + nf) % nf
        remote(err.at[frm], err.at[frm], er_send.at[d], er_recv.at[d], (l, frm)).wait_recv()
    err_out[...] = err[...].astype(F32).reshape(tokens, width).astype(BF16)

    def grad(c):
        sl = pl.ds(pl.multiple_of(c * fl, fl), fl)
        return lax.dot_general(
            err_out[...], dw[sl, :], (((1,), (1,)), ((), ())), preferred_element_type=F32
        )

    if li_n == 2:

        def g_step1(d, _):
            o = (lo + d + 1) % lo_n
            g_send1[o] = grad(o * li_n + 1 - li).astype(BF16)
            remote(g_send1.at[o], g_recv1.at[o], q1_send.at[o], q1_recv.at[o], (lpeer, f)).start()
            return 0

        lax.fori_loop(0, lo_n, g_step1, 0)

    def peer_part(o):
        remote(g_recv1.at[o], g_recv1.at[o], q1_send.at[o], q1_recv.at[o], (lpeer, f)).wait_recv()
        return g_recv1[o].astype(F32)

    def g_step2(d, _):
        o = (lo + d) % lo_n
        g = grad(o * li_n + li)
        if li_n == 2:
            g = g + peer_part(o)
        g_send2[d] = g.astype(BF16)
        remote(g_send2.at[d], g_recv2.at[d], q2_send.at[d], q2_recv.at[d], (o * li_n + li, f)).start()
        return 0

    lax.fori_loop(1, lo_n, g_step2, 0)

    tot = sq_send[...]
    for d in range(1, nf):
        remote(sq_recv.at[d], sq_recv.at[d], sq_ssem.at[d], sq_rsem.at[d], (l, f)).wait_recv()
        tot = tot + sq_recv[d]
    tot_send[...] = tot
    for d in range(1, nl):
        send(tot_send, tot_recv.at[d], tt_ssem.at[d], tt_rsem.at[d], ((l + d) % nl, f))

    g = grad(l)
    if li_n == 2:
        g = g + peer_part(lo)
    _, pullback = jax.vjp(jax.nn.gelu, preact[...])
    for d in range(1, nl):
        remote(tot_recv.at[d], tot_recv.at[d], tt_ssem.at[d], tt_rsem.at[d], (l, f)).wait_recv()
        tot = tot + tot_recv[d]
    mse_out[...] = tot * mse_scale
    for d in range(1, lo_n):
        remote(g_recv2.at[d], g_recv2.at[d], q2_send.at[d], q2_recv.at[d], (l, f)).wait_recv()
        g = g + g_recv2[d].astype(F32)
    pre_out[...] = pullback(g)[0].astype(BF16)

    for c in sends:
        c.wait_send()
    for d in range(1, lo_n):
        remote(g_send2.at[d], g_recv2.at[d], q2_send.at[d], q2_recv.at[d], (l, f)).wait_send()
        if li_n == 2:
            b = ((lo - d + lo_n) % lo_n) * li_n + li
            remote(feats_out.at[b], feats_out.at[b], fb_send.at[d], fb_recv.at[d], (lpeer, f)).wait_send()
    if li_n == 2:
        for o in range(lo_n):
            remote(g_send1.at[o], g_recv1.at[o], q1_send.at[o], q1_recv.at[o], (lpeer, f)).wait_send()


def outer_kernel(n1, a1_ref, b1_ref, a2_ref, b2_ref, o1_ref, o2_ref):
    i = pl.program_id(0)
    dims = (((0,), (0,)), ((), ()))

    @pl.when(i < n1)
    def _():
        o1_ref[...] = lax.dot_general(a1_ref[0], b1_ref[...], dims, preferred_element_type=F32).astype(BF16)

    @pl.when(i >= n1)
    def _():
        o2_ref[...] = lax.dot_general(a2_ref[0], b2_ref[...], dims, preferred_element_type=F32).astype(BF16)


def per_device(sources, targets, enc_weight, enc_bias, dec_weight, dec_bias):
    nl, nf = lax.axis_size("layer"), lax.axis_size("feat")
    lo_n, _ = split2(nl)
    fo_n, _ = split2(nf)
    r, depth = sources.shape
    tokens = r * nl * nf
    fl = enc_weight.shape[1]
    block, width = dec_weight.shape
    tf = tokens // nf
    kw = 1024
    nk = depth // kw
    per, cper = depth // LANES, width // LANES
    src = sources.reshape(r * per, LANES)
    tgt = targets.reshape(r, nl, cper, LANES).transpose(1, 0, 2, 3).reshape(nl, r * cper, LANES)
    dma = pltpu.SemaphoreType.DMA
    vmem = pl.BlockSpec(memory_space=pltpu.VMEM)
    hbm = pl.BlockSpec(memory_space=pl.ANY)
    sds = jax.ShapeDtypeStruct
    x, feats, errors, pre_grad, mse = pl.pallas_call(
        functools.partial(
            gather_kernel, nl, nf, 1.0 / math.sqrt(tokens), 1.0 / (tokens * nl * width)
        ),
        out_shape=(
            sds((nk, tokens, kw), BF16),
            sds((nl, tokens, fl), BF16),
            sds((tokens, width), BF16),
            sds((tokens, fl), BF16),
            sds((8, LANES), F32),
        ),
        in_specs=[vmem, vmem, vmem, vmem, hbm, hbm],
        out_specs=(vmem,) * 5,
        scratch_shapes=[
            pltpu.VMEM((depth, fl), BF16),
            pltpu.VMEM((block, width), BF16),
            pltpu.VMEM((nf, nl, r * per, LANES), BF16),
            pltpu.VMEM((tokens * per, LANES), F32),
            pltpu.VMEM((nl, r * cper, LANES), BF16),
            pltpu.VMEM((tf * cper, LANES), F32),
            pltpu.VMEM((tokens, fl), F32),
            pltpu.VMEM((tokens, width), F32),
            pltpu.VMEM((nf, tf, width), BF16),
            pltpu.VMEM((nf, tf, width), BF16),
            pltpu.VMEM((nf, tf, width), BF16),
            pltpu.VMEM((lo_n, tokens, fl), BF16),
            pltpu.VMEM((lo_n, tokens, fl), BF16),
            pltpu.VMEM((lo_n, tokens, fl), BF16),
            pltpu.VMEM((lo_n, tokens, fl), BF16),
            pltpu.VMEM((8, LANES), F32),
            pltpu.VMEM((nf, 8, LANES), F32),
            pltpu.VMEM((8, LANES), F32),
            pltpu.VMEM((nl, 8, LANES), F32),
            dma((nk,)), dma((nl,)),
            dma((nl,)), dma((nl,)), dma((fo_n,)), dma((fo_n,)), dma((fo_n,)), dma((fo_n,)),
            dma((nl,)), dma((nl,)),
            dma((lo_n,)), dma((lo_n,)), dma((lo_n,)), dma((lo_n,)),
            dma((nf,)), dma((nf,)), dma((nf,)), dma((nf,)),
            dma((lo_n,)), dma((lo_n,)), dma((lo_n,)), dma((lo_n,)),
            dma((nf,)), dma((nf,)), dma((nl,)), dma((nl,)),
        ],
        compiler_params=pltpu.CompilerParams(
            collective_id=0, has_side_effects=True, vmem_limit_bytes=62 * 2**20
        ),
        name="gather",
    )(src, tgt, enc_bias.reshape(1, fl), dec_bias.reshape(1, width), enc_weight, dec_weight)

    rb1 = min(512, fl)
    rb2 = min(1024, kw)
    n1, n2 = block // rb1, depth // rb2
    p1, p2 = fl // rb1, kw // rb2

    def i1(i):
        return jnp.minimum(i, n1 - 1)

    def i2(i):
        return jnp.maximum(i - n1, 0)

    dec_grad, enc_grad = pl.pallas_call(
        functools.partial(outer_kernel, n1),
        grid=(n1 + n2,),
        out_shape=(sds((block, width), BF16), sds((depth, fl), BF16)),
        in_specs=[
            pl.BlockSpec((1, tokens, rb1), lambda i: (i1(i) // p1, 0, i1(i) % p1)),
            pl.BlockSpec((tokens, width), lambda i: (0, 0)),
            pl.BlockSpec((1, tokens, rb2), lambda i: (i2(i) // p2, 0, i2(i) % p2)),
            pl.BlockSpec((tokens, fl), lambda i: (0, 0)),
        ],
        out_specs=(
            pl.BlockSpec((rb1, width), lambda i: (i1(i), 0)),
            pl.BlockSpec((rb2, fl), lambda i: (i2(i), 0)),
        ),
        compiler_params=pltpu.CompilerParams(vmem_limit_bytes=48 * 2**20),
        name="outer",
    )(feats, errors, x, pre_grad)
    return (enc_grad, dec_grad, mse[0, 0])


def solution(mesh):
    return jax.shard_map(
        per_device,
        mesh=mesh,
        in_specs=(
            P(("layer", "feat"), None),
            P(("layer", "feat"), None),
            P(None, ("feat", "layer")),
            P(("feat", "layer")),
            P("feat", "layer"),
            P("layer"),
        ),
        out_specs=(P(None, ("feat", "layer")), P("feat", "layer"), P()),
        check_vma=False,
    )
```

```python
import functools
import math

import jax
import jax.numpy as jnp
from jax import lax
from jax.experimental import pallas as pl
from jax.experimental.pallas import tpu as pltpu
from jax.sharding import PartitionSpec as P

MESH = pl.DeviceIdType.MESH
BF16 = jnp.bfloat16
F32 = jnp.float32
LANES = 128


def split2(n):
    return (n // 2, 2) if n % 2 == 0 else (n, 1)


def gather_kernel(
    nl, nf, scale, mse_scale,
    src_in, tgt_in, ebias_ref, dbias_ref, ew_hbm, dw_hbm,
    x_out, feats_out, err_out, pre_out, mse_out,
    ew, dw, rows, rows32, tgt_ref, tgt_stage, tgts, tgt32, preact, part, rs_send, rs_recv, err,
    g_send1, g_recv1, g_send2, g_recv2, sq_send, sq_recv, tot_send, tot_recv,
    ew_sem, dw_sem,
    s1_send, s1_recv, s2_send, s2_recv, s3_send, s3_recv, t_send, t_recv,
    fa_send, fa_recv, fb_send, fb_recv, rs_ssem, rs_rsem, er_send, er_recv,
    q1_send, q1_recv, q2_send, q2_recv, sq_ssem, sq_rsem, tt_ssem, tt_rsem,
):
    lo_n, li_n = split2(nl)
    fo_n, fi_n = split2(nf)
    l = lax.axis_index("layer")
    f = lax.axis_index("feat")
    lo, li = l // li_n, l % li_n
    fo, fi = f // fi_n, f % fi_n
    nk, tokens, kw = x_out.shape
    fl = feats_out.shape[2]
    tf = tokens // nf
    width = dw.shape[1]

    per = nk * kw // LANES
    cper = width // LANES
    for k in range(nk):
        pltpu.make_async_copy(ew_hbm.at[pl.ds(k * kw, kw)], ew.at[pl.ds(k * kw, kw)], ew_sem.at[k]).start()

    def dw_copy(c):
        sl = pl.ds(pl.multiple_of(c * fl, fl), fl)
        return pltpu.make_async_copy(dw_hbm.at[sl], dw.at[sl], dw_sem.at[c])

    r = src_in.shape[0]
    own_rows = src_in[...].astype(F32)
    for i in range(r):
        for s in range(per):
            rows32[i * per + s : i * per + s + 1, :] = own_rows[i : i + 1, s * LANES : (s + 1) * LANES]
    own_tgt = tgt_in[...].astype(F32)
    for c in range(nl):
        for i in range(r):
            for s in range(cper):
                col = (c * cper + s) * LANES
                row = i * cper + s
                tgt_stage[c, row : row + 1, :] = own_tgt[i : i + 1, col : col + LANES]
    tgt_ref[...] = tgt_stage[...].astype(BF16)
    rows[f, l] = rows32[: r * per, :].astype(BF16)

    barrier = pltpu.get_barrier_semaphore()
    for d in range(1, nl):
        pl.semaphore_signal(barrier, inc=1, device_id=((l + d) % nl, f), device_id_type=MESH)
    for d in range(1, nf):
        pl.semaphore_signal(barrier, inc=1, device_id=(l, (f + d) % nf), device_id_type=MESH)
    pl.semaphore_wait(barrier, nl - 1 + nf - 1)

    def remote(src, dst, ssem, rsem, dev):
        return pltpu.make_async_remote_copy(
            src_ref=src, dst_ref=dst, send_sem=ssem, recv_sem=rsem, device_id=dev, device_id_type=MESH
        )

    sends = []

    def send(src, dst, ssem, rsem, dev):
        c = remote(src, dst, ssem, rsem, dev)
        c.start()
        sends.append(c)

    for d in range(1, nl):
        to = (l + d) % nl
        send(rows.at[f, l], rows.at[f, l], s1_send.at[d], s1_recv.at[d], (to, f))
    for d in range(1, nl):
        to = (l + d) % nl
        send(tgt_ref.at[to], tgts.at[l], t_send.at[d], t_recv.at[d], (to, f))
    for c in range(nl):
        dw_copy(c).start()
    for d in range(1, nl):
        frm = (l - d + nl) % nl
        remote(rows.at[f, frm], rows.at[f, frm], s1_send.at[d], s1_recv.at[d], (frm, f)).wait_recv()
    for d in range(1, fo_n):
        to = ((fo + d) % fo_n) * fi_n + fi
        send(rows.at[f], rows.at[f], s2_send.at[d], s2_recv.at[d], (l, to))
    if fi_n == 2:
        peer = fo * fi_n + 1 - fi
        send(rows.at[f], rows.at[f], s3_send.at[0], s3_recv.at[0], (l, peer))
    for d in range(1, fo_n):
        b = ((fo - d + fo_n) % fo_n) * fi_n + fi
        remote(rows.at[b], rows.at[b], s2_send.at[d], s2_recv.at[d], (l, b)).wait_recv()
        if fi_n == 2:
            send(rows.at[b], rows.at[b], s3_send.at[d], s3_recv.at[d], (l, peer))
    if fi_n == 2:
        for d in range(fo_n):
            b = ((fo - d + fo_n) % fo_n) * fi_n + 1 - fi
            remote(rows.at[b], rows.at[b], s3_send.at[d], s3_recv.at[d], (l, peer)).wait_recv()
    rows32[...] = rows[...].astype(F32).reshape(tokens * per, LANES)
    for s in range(per):
        at = s * LANES
        x_out[at // kw, :, at % kw : at % kw + LANES] = rows32[pl.ds(s, tokens, stride=per), :].astype(BF16)

    preact[...] = jnp.broadcast_to(ebias_ref[...], preact.shape)

    def enc_step(k, _):
        sl = pl.ds(pl.multiple_of(k * kw, kw), kw)
        pltpu.make_async_copy(ew_hbm.at[sl], ew.at[sl], ew_sem.at[k]).wait()
        preact[...] += jnp.dot(x_out[k], ew[sl, :], preferred_element_type=F32)
        return 0

    lax.fori_loop(0, nk, enc_step, 0)
    feats_out[l] = jax.nn.gelu(preact[...]).astype(BF16)

    for d in range(1, lo_n):
        to = ((lo + d) % lo_n) * li_n + li
        send(feats_out.at[l], feats_out.at[l], fa_send.at[d], fa_recv.at[d], (to, f))
    lpeer = lo * li_n + 1 - li
    if li_n == 2:
        send(feats_out.at[l], feats_out.at[l], fb_send.at[0], fb_recv.at[0], (lpeer, f))
    part[...] = jnp.zeros_like(part)

    def decode(c):
        dw_copy(c).wait()
        sl = pl.ds(pl.multiple_of(c * fl, fl), fl)
        part[...] += jnp.dot(feats_out[c], dw[sl, :], preferred_element_type=F32)

    def dec_step(d, _):
        b = ((lo - d + lo_n) % lo_n) * li_n + li

        @pl.when(d > 0)
        def _():
            remote(feats_out.at[b], feats_out.at[b], fa_send.at[d], fa_recv.at[d], (b, f)).wait_recv()
            if li_n == 2:
                remote(feats_out.at[b], feats_out.at[b], fb_send.at[d], fb_recv.at[d], (lpeer, f)).start()

        decode(b)
        return 0

    lax.fori_loop(0, lo_n, dec_step, 0)
    if li_n == 2:

        def dec_step2(d, _):
            b = ((lo - d + lo_n) % lo_n) * li_n + 1 - li
            remote(feats_out.at[b], feats_out.at[b], fb_send.at[d], fb_recv.at[d], (lpeer, f)).wait_recv()
            decode(b)
            return 0

        lax.fori_loop(0, lo_n, dec_step2, 0)

    tgts[l] = tgt_ref[l]
    for d in range(1, nl):
        frm = (l - d + nl) % nl
        remote(tgts.at[frm], tgts.at[frm], t_send.at[d], t_recv.at[d], (frm, f)).wait_recv()
    tgt32[...] = tgts[...].astype(F32).reshape(tf * cper, LANES)

    rs_send[...] = part[...].reshape(nf, tf, width).astype(BF16)
    for d in range(1, nf):
        to = (f + d) % nf
        send(rs_send.at[to], rs_recv.at[d], rs_ssem.at[d], rs_rsem.at[d], (l, to))
    own = part[pl.ds(pl.multiple_of(f * tf, tf), tf), :]
    own = own + dbias_ref[...]
    want = jnp.concatenate([tgt32[pl.ds(s, tf, stride=cper), :] for s in range(cper)], axis=1)
    for d in range(1, nf):
        remote(rs_recv.at[d], rs_recv.at[d], rs_ssem.at[d], rs_rsem.at[d], (l, f)).wait_recv()
        own = own + rs_recv[d].astype(F32)
    misfit = own - want
    err[f] = (misfit * scale).astype(BF16)
    for d in range(1, nf):
        to = (f + d) % nf
        send(err.at[f], err.at[f], er_send.at[d], er_recv.at[d], (l, to))
    sq = jnp.sum(misfit * misfit)
    sq_send[...] = jnp.full(sq_send.shape, sq, F32)
    for d in range(1, nf):
        to = (f + d) % nf
        send(sq_send, sq_recv.at[d], sq_ssem.at[d], sq_rsem.at[d], (l, to))
    for d in range(1, nf):
        frm = (f - d + nf) % nf
        remote(err.at[frm], err.at[frm], er_send.at[d], er_recv.at[d], (l, frm)).wait_recv()
    err_out[...] = err[...].astype(F32).reshape(tokens, width).astype(BF16)

    def grad(c):
        sl = pl.ds(pl.multiple_of(c * fl, fl), fl)
        return lax.dot_general(
            err_out[...], dw[sl, :], (((1,), (1,)), ((), ())), preferred_element_type=F32
        )

    if li_n == 2:

        def g_step1(d, _):
            o = (lo + d + 1) % lo_n
            g_send1[o] = grad(o * li_n + 1 - li).astype(BF16)
            remote(g_send1.at[o], g_recv1.at[o], q1_send.at[o], q1_recv.at[o], (lpeer, f)).start()
            return 0

        lax.fori_loop(0, lo_n, g_step1, 0)

    def peer_part(o):
        remote(g_recv1.at[o], g_recv1.at[o], q1_send.at[o], q1_recv.at[o], (lpeer, f)).wait_recv()
        return g_recv1[o].astype(F32)

    def g_step2(d, _):
        o = (lo + d) % lo_n
        g = grad(o * li_n + li)
        if li_n == 2:
            g = g + peer_part(o)
        g_send2[d] = g.astype(BF16)
        remote(g_send2.at[d], g_recv2.at[d], q2_send.at[d], q2_recv.at[d], (o * li_n + li, f)).start()
        return 0

    lax.fori_loop(1, lo_n, g_step2, 0)

    tot = sq_send[...]
    for d in range(1, nf):
        remote(sq_recv.at[d], sq_recv.at[d], sq_ssem.at[d], sq_rsem.at[d], (l, f)).wait_recv()
        tot = tot + sq_recv[d]
    tot_send[...] = tot
    for d in range(1, nl):
        send(tot_send, tot_recv.at[d], tt_ssem.at[d], tt_rsem.at[d], ((l + d) % nl, f))

    g = grad(l)
    if li_n == 2:
        g = g + peer_part(lo)
    _, pullback = jax.vjp(jax.nn.gelu, preact[...])
    for d in range(1, nl):
        remote(tot_recv.at[d], tot_recv.at[d], tt_ssem.at[d], tt_rsem.at[d], (l, f)).wait_recv()
        tot = tot + tot_recv[d]
    mse_out[...] = tot * mse_scale
    for d in range(1, lo_n):
        remote(g_recv2.at[d], g_recv2.at[d], q2_send.at[d], q2_recv.at[d], (l, f)).wait_recv()
        g = g + g_recv2[d].astype(F32)
    pre_out[...] = pullback(g)[0].astype(BF16)

    for c in sends:
        c.wait_send()
    for d in range(1, lo_n):
        remote(g_send2.at[d], g_recv2.at[d], q2_send.at[d], q2_recv.at[d], (l, f)).wait_send()
        if li_n == 2:
            b = ((lo - d + lo_n) % lo_n) * li_n + li
            remote(feats_out.at[b], feats_out.at[b], fb_send.at[d], fb_recv.at[d], (lpeer, f)).wait_send()
    if li_n == 2:
        for o in range(lo_n):
            remote(g_send1.at[o], g_recv1.at[o], q1_send.at[o], q1_recv.at[o], (lpeer, f)).wait_send()


def outer_kernel(a1_ref, b1_ref, a2_ref, b2_ref, m_ref, o1_hbm, o2_hbm, o3_ref, o1, o2, sem1, sem2):
    dims = (((0,), (0,)), ((), ()))
    o3_ref[0, 0] = jnp.max(m_ref[...])

    def copy(out, hbm, sem, j, n):
        sl = pl.ds(pl.multiple_of(j * n, n), n)
        return pltpu.make_async_copy(out.at[sl], hbm.at[sl], sem.at[j])

    def run(left, right, out, hbm, sem):
        count, _, n = left.shape

        def step(j, _):
            out[pl.ds(pl.multiple_of(j * n, n), n), :] = lax.dot_general(
                left[j], right[...], dims, preferred_element_type=F32
            ).astype(BF16)
            copy(out, hbm, sem, j, n).start()
            return 0

        lax.fori_loop(0, count, step, 0)

    def finish(left, out, hbm, sem):
        count, _, n = left.shape

        def step(j, _):
            copy(out, hbm, sem, j, n).wait()
            return 0

        lax.fori_loop(0, count, step, 0)

    run(a2_ref, b2_ref, o2, o2_hbm, sem2)
    run(a1_ref, b1_ref, o1, o1_hbm, sem1)
    finish(a2_ref, o2, o2_hbm, sem2)
    finish(a1_ref, o1, o1_hbm, sem1)


def outer(feats, errors, x, pre_grad, mse):
    nl, tokens, fl = feats.shape
    nk, _, kw = x.shape
    width = errors.shape[1]
    vmem = pl.BlockSpec(memory_space=pltpu.VMEM)
    hbm = pl.BlockSpec(memory_space=pl.ANY)
    sds = jax.ShapeDtypeStruct
    return pl.pallas_call(
        outer_kernel,
        out_shape=(sds((nl * fl, width), BF16), sds((nk * kw, fl), BF16), sds((1, 1), F32)),
        in_specs=[vmem] * 5,
        out_specs=(hbm, hbm, pl.BlockSpec(memory_space=pltpu.SMEM)),
        scratch_shapes=[
            pltpu.VMEM((nl * fl, width), BF16),
            pltpu.VMEM((nk * kw, fl), BF16),
            pltpu.SemaphoreType.DMA((nl,)),
            pltpu.SemaphoreType.DMA((nk,)),
        ],
        compiler_params=pltpu.CompilerParams(vmem_limit_bytes=62 * 2**20),
        name="outer",
    )(feats, errors, x, pre_grad, mse)


def per_device(sources, targets, enc_weight, enc_bias, dec_weight, dec_bias):
    nl, nf = lax.axis_size("layer"), lax.axis_size("feat")
    lo_n, _ = split2(nl)
    fo_n, _ = split2(nf)
    r, depth = sources.shape
    tokens = r * nl * nf
    fl = enc_weight.shape[1]
    block, width = dec_weight.shape
    tf = tokens // nf
    kw = 1024
    nk = depth // kw
    per, cper = depth // LANES, width // LANES
    dma = pltpu.SemaphoreType.DMA
    vmem = pl.BlockSpec(memory_space=pltpu.VMEM)
    hbm = pl.BlockSpec(memory_space=pl.ANY)
    sds = jax.ShapeDtypeStruct
    x, feats, errors, pre_grad, mse = pl.pallas_call(
        functools.partial(
            gather_kernel, nl, nf, 1.0 / math.sqrt(tokens), 1.0 / (tokens * nl * width)
        ),
        out_shape=(
            sds((nk, tokens, kw), BF16),
            sds((nl, tokens, fl), BF16),
            sds((tokens, width), BF16),
            sds((tokens, fl), BF16),
            sds((8, LANES), F32),
        ),
        in_specs=[vmem, vmem, vmem, vmem, hbm, hbm],
        out_specs=(vmem,) * 5,
        scratch_shapes=[
            pltpu.VMEM((depth, fl), BF16),
            pltpu.VMEM((block, width), BF16),
            pltpu.VMEM((nf, nl, r * per, LANES), BF16),
            pltpu.VMEM((tokens * per, LANES), F32),
            pltpu.VMEM((nl, r * cper, LANES), BF16),
            pltpu.VMEM((nl, r * cper, LANES), F32),
            pltpu.VMEM((nl, r * cper, LANES), BF16),
            pltpu.VMEM((tf * cper, LANES), F32),
            pltpu.VMEM((tokens, fl), F32),
            pltpu.VMEM((tokens, width), F32),
            pltpu.VMEM((nf, tf, width), BF16),
            pltpu.VMEM((nf, tf, width), BF16),
            pltpu.VMEM((nf, tf, width), BF16),
            pltpu.VMEM((lo_n, tokens, fl), BF16),
            pltpu.VMEM((lo_n, tokens, fl), BF16),
            pltpu.VMEM((lo_n, tokens, fl), BF16),
            pltpu.VMEM((lo_n, tokens, fl), BF16),
            pltpu.VMEM((8, LANES), F32),
            pltpu.VMEM((nf, 8, LANES), F32),
            pltpu.VMEM((8, LANES), F32),
            pltpu.VMEM((nl, 8, LANES), F32),
            dma((nk,)), dma((nl,)),
            dma((nl,)), dma((nl,)), dma((fo_n,)), dma((fo_n,)), dma((fo_n,)), dma((fo_n,)),
            dma((nl,)), dma((nl,)),
            dma((lo_n,)), dma((lo_n,)), dma((lo_n,)), dma((lo_n,)),
            dma((nf,)), dma((nf,)), dma((nf,)), dma((nf,)),
            dma((lo_n,)), dma((lo_n,)), dma((lo_n,)), dma((lo_n,)),
            dma((nf,)), dma((nf,)), dma((nl,)), dma((nl,)),
        ],
        compiler_params=pltpu.CompilerParams(
            collective_id=0, has_side_effects=True, vmem_limit_bytes=62 * 2**20
        ),
        name="gather",
    )(sources, targets, enc_bias.reshape(1, fl), dec_bias.reshape(1, width), enc_weight, dec_weight)

    dec_grad, enc_grad, mean_sq = outer(feats, errors, x, pre_grad, mse)
    return (enc_grad, dec_grad, mean_sq.reshape(()))


def solution(mesh):
    return jax.shard_map(
        per_device,
        mesh=mesh,
        in_specs=(
            P(("layer", "feat"), None),
            P(("layer", "feat"), None),
            P(None, ("feat", "layer")),
            P(("feat", "layer")),
            P("feat", "layer"),
            P("layer"),
        ),
        out_specs=(P(None, ("feat", "layer")), P("feat", "layer"), P()),
        check_vma=False,
    )
```
